32 devices in a mesh: section: 4 (over y, core), shard: 8 (over z, x).
Axes of the slice: x: 2, y: 2, z: 4, core: 2. Of those that a mesh axis runs over, the one named last changes fastest.
Arguments:
- train_weights: float32 [4, 16384, 1024], P('section', 'shard'), may hold values from -0.046875 to 0.046875
- section_to_group: int32 [4], replicated, may hold values from 0 to 3, each once
- hidden: bfloat16 [512, 16384], P(('section', 'shard')), may hold values from -6 to 6
- queries: bfloat16 [2048, 2048], P(('section', 'shard')), may hold values from -100 to 100
- kv_cache: bfloat16 [2048, 128, 256], P(('section', 'shard')), may hold values from -5 to 5
- lengths: int32 [512], P('section'), may hold values from 2 to 127, as said below
Outputs:
- context: bfloat16 [2048, 2048], P(('section', 'shard'))
- layer_out: bfloat16 [4, 4, 256, 16384], P('section', None, 'shard')
The draws below stay inside these ranges and needn't reach their ends.
Inputs may be any that keep to these rules, and one draw needn't show every extreme that they name: `section_to_group`: a permutation: each rollout group runs exactly one trainer section's layer. `lengths`: every row has at least two cached tokens; some row of every device has 127.
All inputs are finite; a program needn't handle non-finite values.
Results may differ from the reference program's by a relative error of at most 0.006.
Values may be sent and summed in bfloat16 or wider, within the bound.
A program may use at most 64 MiB of HBM per device.

```python
import math
import jax
import jax.numpy as jnp
from jax import lax

D = 16384
HD = 128
QPK = 16
KVH = 4
LEN = 128
ROWS = 128
KVC = 1024
N_SECTION = 4


def cache_values(key):
    entries = N_SECTION * KVH * ROWS
    drawn = jax.random.normal(jax.random.fold_in(key, 101), (entries, LEN, 2 * HD), jnp.float32)
    drawn = jnp.clip(drawn, -5.0, 5.0)
    return drawn


def draw_kv_cache(key, part):
    return cache_values(key).astype(jnp.bfloat16)


def draw_queries(key, part):
    entries = N_SECTION * KVH * ROWS
    drawn = jax.random.normal(jax.random.fold_in(key, 202), (entries, QPK * HD), jnp.float32)
    drawn = jnp.clip(drawn, -5.0, 5.0)
    return drawn.astype(jnp.bfloat16)


def draw_lengths(key, part):
    count = N_SECTION * ROWS
    drawn = jax.random.randint(jax.random.fold_in(key, 303), (count,), 2, LEN)
    return jnp.where(jnp.arange(count) % 5 == 0, LEN - 1, drawn).astype(jnp.int32)


def block_levels(stream_key, dims, shards, low, high):
    factor_of = 1.0
    for position, blocks in shards:
        draws = jax.random.uniform(jax.random.fold_in(jax.random.fold_in(stream_key, 6), position), (blocks,), jnp.float32, low / len(shards), high / len(shards))
        factor_of = factor_of * jnp.repeat(jnp.exp(draws), dims[position] // blocks).reshape((-1,) + (1,) * (len(dims) - 1 - position))
    return factor_of


def noise(stream_key, dims, deviation, reach, cuts=(), kind=jnp.bfloat16):
    values = deviation * jax.random.normal(stream_key, dims, jnp.float32)
    if cuts:
        values = values * block_levels(stream_key, dims, cuts, -0.22, 0.18)
    return jnp.clip(values, -reach, reach).astype(kind)


def setup_inputs(seed: int = 0) -> dict:
    arg_keys = jax.random.split(jax.random.key(seed), 7)
    return {
        "train_weights": noise(arg_keys[0], (N_SECTION, D, KVC), D ** -0.5, 0.046875, ((0, 4), (1, 8)), jnp.float32),
        "section_to_group": jax.random.permutation(arg_keys[1], N_SECTION).astype(jnp.int32),
        "hidden": noise(arg_keys[2], (N_SECTION * ROWS, D), 1.0, 6.0, ((0, 32),)),
        "queries": draw_queries(jax.random.fold_in(arg_keys[6], 71), 0),
        "kv_cache": draw_kv_cache(jax.random.fold_in(arg_keys[6], 71), 0),
        "lengths": draw_lengths(jax.random.fold_in(arg_keys[6], 71), 0),
    }


def attend(query_rows, cache_rows, fresh_rows, row_lengths):
    score_scale = 1.0 / math.sqrt(HD)
    query_f = query_rows.astype(jnp.float32)
    cached_keys = cache_rows[:, :, :HD].astype(jnp.float32)
    cached_values = cache_rows[:, :, HD:].astype(jnp.float32)
    key_new = fresh_rows[:, :HD].astype(jnp.float32)
    value_new = fresh_rows[:, HD:].astype(jnp.float32)
    scores = jnp.einsum('rhd,rtd->rht', query_f, cached_keys) * score_scale
    valid = jnp.arange(LEN)[None, None, :] < row_lengths[:, None, None]
    scores = jnp.where(valid, scores, -1e+30)
    fresh_score = jnp.einsum('rhd,rd->rh', query_f, key_new) * score_scale
    highest = jnp.maximum(lax.optimization_barrier(jnp.max(scores, axis=-1)), fresh_score)
    weights = jnp.where(valid, jnp.exp(scores - highest[..., None]), 0.0)
    fresh_weight = jnp.exp(fresh_score - highest)
    total = lax.optimization_barrier(jnp.sum(weights, axis=-1)) + fresh_weight
    probs = (weights / total[..., None]).astype(jnp.bfloat16)
    fresh_prob = (fresh_weight / total).astype(jnp.bfloat16)
    context = jnp.einsum('rht,rtd->rhd', probs.astype(jnp.float32), cached_values)
    context = context + fresh_prob.astype(jnp.float32)[..., None] * value_new[:, None, :]
    return context.reshape(context.shape[0], QPK * HD).astype(jnp.bfloat16)

def reference(train_weights, section_to_group, hidden, queries, kv_cache, lengths):
    source = jnp.argsort(section_to_group).astype(jnp.int32)

    def one_group(group_id):
        layer = lax.dynamic_index_in_dim(train_weights, source[group_id], 0, keepdims=False).astype(jnp.bfloat16)
        inputs = lax.dynamic_slice_in_dim(hidden, group_id * ROWS, ROWS, 0)
        fresh = jnp.dot(inputs, layer, preferred_element_type=jnp.float32).astype(jnp.bfloat16)
        fresh = fresh.reshape(ROWS, KVH, 2 * HD).transpose(1, 0, 2).reshape(KVH * ROWS, 2 * HD)
        query_rows = lax.dynamic_slice_in_dim(queries, group_id * KVH * ROWS, KVH * ROWS, 0).reshape(KVH * ROWS, QPK, HD)
        cache_rows = lax.dynamic_slice_in_dim(kv_cache, group_id * KVH * ROWS, KVH * ROWS, 0)
        row_lengths = jnp.tile(lax.dynamic_slice_in_dim(lengths, group_id * ROWS, ROWS, 0), KVH)
        kept = layer.reshape(D, KVH, 2 * HD).transpose(1, 2, 0)
        return (attend(query_rows, cache_rows, fresh, row_lengths), kept)
    result, layer_out = lax.map(one_group, jnp.arange(N_SECTION, dtype=jnp.int32))
    return (result.reshape(N_SECTION * KVH * ROWS, QPK * HD), layer_out)
```

```python
import functools
import math

import jax
import jax.numpy as jnp
from jax import lax
from jax.experimental import pallas as pl
from jax.experimental.pallas import tpu as pltpu
from jax.sharding import PartitionSpec as P

D = 16384
HD = 128
QPK = 16
KVH = 4
LEN = 128
ROWS = 128


def route(blocks, source):
    spread = lax.all_to_all(blocks, "section", split_axis=2, concat_axis=0, tiled=True)
    picked = jnp.take(spread, source, axis=0)
    return lax.all_to_all(picked, "section", split_axis=0, concat_axis=2, tiled=True)


def attend(query_rows, cache_rows, fresh_rows, row_lengths):
    score_scale = 1.0 / math.sqrt(HD)
    cached_keys = cache_rows[:, :, :HD]
    cached_values = cache_rows[:, :, HD:]
    key_new = fresh_rows[:, :HD]
    value_new = fresh_rows[:, HD:]
    scores = (
        jnp.einsum("rhd,rtd->rht", query_rows, cached_keys, preferred_element_type=jnp.float32)
        * score_scale
    )
    valid = jnp.arange(LEN)[None, None, :] < row_lengths[:, None, None]
    scores = jnp.where(valid, scores, -1e30)
    fresh_score = (
        jnp.einsum("rhd,rd->rh", query_rows, key_new, preferred_element_type=jnp.float32)
        * score_scale
    )
    highest = jnp.maximum(jnp.max(scores, axis=-1), fresh_score)
    weights = jnp.where(valid, jnp.exp(scores - highest[..., None]), 0.0)
    fresh_weight = jnp.exp(fresh_score - highest)
    total = jnp.sum(weights, axis=-1) + fresh_weight
    probs = (weights / total[..., None]).astype(jnp.bfloat16)
    fresh_prob = (fresh_weight / total).astype(jnp.bfloat16)
    context = jnp.einsum("rht,rtd->rhd", probs, cached_values, preferred_element_type=jnp.float32)
    context = (
        context
        + fresh_prob.astype(jnp.float32)[..., None] * value_new.astype(jnp.float32)[:, None, :]
    )
    return context.reshape(context.shape[0], QPK * HD).astype(jnp.bfloat16)


def plain_body(train_weights, section_to_group, hidden, queries, kv_cache, lengths):
    shards = lax.axis_size("shard")
    per_head = shards // KVH
    row_block = ROWS // per_head
    piece_cols = 2 * HD // shards
    source = jnp.argsort(section_to_group)
    flipped = train_weights[0].astype(jnp.bfloat16).T
    slice_rows = flipped.shape[1]
    routed = route(flipped[None], source)[0]
    pieces = routed.reshape(KVH, shards, piece_cols, slice_rows).transpose(1, 0, 2, 3)
    column_block = lax.all_to_all(pieces, "shard", split_axis=0, concat_axis=3, tiled=True)
    column_block = column_block.reshape(KVH * piece_cols, D)
    feature_block = lax.all_to_all(hidden, "shard", split_axis=1, concat_axis=0, tiled=True)
    partial_value = lax.dot_general(
        feature_block, routed, (((1,), (1,)), ((), ())), preferred_element_type=jnp.float32
    )
    arranged = partial_value.reshape(per_head, row_block, KVH, 2 * HD).transpose(2, 0, 1, 3)
    arranged = arranged.reshape(shards * row_block, 2 * HD)
    fresh = lax.psum_scatter(arranged, "shard", scatter_dimension=0, tiled=True).astype(
        jnp.bfloat16
    )
    position = lax.axis_index("shard")
    block_index = position % per_head
    row_lengths = lax.dynamic_slice_in_dim(lengths, block_index * row_block, row_block, 0)
    query_rows = queries.reshape(row_block, QPK, HD)
    context = attend(query_rows, kv_cache, fresh, row_lengths)
    layer_out = column_block.reshape(1, KVH, piece_cols, D)
    return (context, layer_out)


def flip(index, mask, size):
    result, bit = 0, 1
    while bit < size:
        value = (index // bit) % 2
        if mask & bit:
            value = 1 - value
        result = result + value * bit
        bit *= 2
    return result


def move_kernel(sections, shards, source_ref, w_ref, hidden_ref, out_ref, fresh_ref, *scratch):
    spread = scratch[:shards]
    (stage, picked, feat, part, part_send, part_recv,
     a_send, a_recv, b_send, b_recv, c_send, c_recv, h_send, h_recv, p_send, p_recv, local) = scratch[shards:]
    me = lax.axis_index("section")
    pos = lax.axis_index("shard")
    heads, _, piece, width = w_ref.shape
    rows_in = hidden_ref.shape[0]
    per_head = shards // heads
    row_block = ROWS // per_head

    barrier = pltpu.get_barrier_semaphore()
    for j in range(1, sections):
        pl.semaphore_signal(barrier, inc=1, device_id={"section": flip(me, j, sections)}, device_id_type=pl.DeviceIdType.MESH)
    for j in range(1, shards):
        pl.semaphore_signal(barrier, inc=1, device_id={"shard": flip(pos, j, shards)}, device_id_type=pl.DeviceIdType.MESH)
    pl.semaphore_wait(barrier, sections + shards - 2)

    def remote(src, dst, send, recv, **target):
        return pltpu.make_async_remote_copy(
            src_ref=src, dst_ref=dst, send_sem=send, recv_sem=recv,
            device_id=target, device_id_type=pl.DeviceIdType.MESH)

    masks = list(range(shards - 1, -1, -1))

    def spread_copies(k):
        p = flip(pos, masks[k], shards)
        copies = []
        for j in range(1, sections):
            t = flip(me, j, sections)
            copies.append(remote(w_ref.at[t, p], spread[k].at[me], a_send.at[k, j], a_recv.at[k, j], section=t))
        return copies

    def collect_copies(k):
        copies = []
        for j in range(1, sections):
            t = flip(me, j, sections)
            copies.append(remote(stage.at[k, t], picked.at[k, me], b_send.at[k, j], b_recv.at[k, j], section=t))
        return copies

    columns = pl.ds(pl.multiple_of(pos * width, width), width)

    def keep_copy(k):
        p = flip(pos, masks[k], shards)
        if masks[k] == 0:
            return pltpu.make_async_copy(picked.at[k], out_ref.at[:, :, columns], local)
        return remote(picked.at[k], out_ref.at[:, :, columns], c_send.at[k], c_recv.at[k], shard=p)

    def hidden_copy(j):
        p = flip(pos, j, shards)
        return remote(hidden_ref.at[:, pl.ds(pl.multiple_of(p * width, width), width)], feat.at[pos],
                      h_send.at[j], h_recv.at[j], shard=p)

    def start_spread(k):
        for copy in spread_copies(k):
            copy.start()
        spread[k][me] = w_ref[me, flip(pos, masks[k], shards)]

    ahead = AHEAD
    for k in range(min(ahead, shards)):
        start_spread(k)
    for j in range(1, shards):
        hidden_copy(j).start()
    feat[pos] = hidden_ref[:, columns]

    def collect(k):
        for copy in spread_copies(k):
            copy.wait()
        for g in range(sections):
            stage[k, g] = spread[k][source_ref[g]]
        picked[k, me] = stage[k, me]
        for copy in collect_copies(k):
            copy.start()

    def forward(k):
        for copy in collect_copies(k):
            copy.wait()
        keep_copy(k).start()
        if k == 0:
            for j in range(1, shards):
                hidden_copy(j).wait()
        p = flip(pos, masks[k], shards)
        value = lax.dot_general(
            picked[k].reshape(heads * piece, width), feat[...].reshape(shards * rows_in, width),
            (((1,), (1,)), ((), ())), preferred_element_type=jnp.float32)
        for h in range(heads):
            part[h, pl.ds(pl.multiple_of(p * piece, piece), piece), :] = value[h * piece:(h + 1) * piece]

    for k in range(shards):
        collect(k)
        if k + ahead < shards:
            start_spread(k + ahead)
        if k >= 1:
            forward(k - 1)
    forward(shards - 1)

    for h in range(heads):
        turned = part[h].T
        for b in range(per_head):
            part_send[h * per_head + b] = turned[b * row_block:(b + 1) * row_block]

    def part_copy(j):
        p = flip(pos, j, shards)
        return remote(part_send.at[p], part_recv.at[j], p_send.at[j], p_recv.at[j], shard=p)

    for j in range(shards - 1, 0, -1):
        part_copy(j).start()
    total = part_send[pos]
    for j in range(1, shards):
        part_copy(j).wait()
        total = total + part_recv[j]
    fresh_ref[...] = total.astype(fresh_ref.dtype)
    for k in range(shards):
        keep_copy(k).wait()


AHEAD = 3


def move(weights, hidden, source):
    sections, shards = lax.axis_size("section"), lax.axis_size("shard")
    heads, _, piece, width = weights.shape
    rows_in = hidden.shape[0]
    row_block = ROWS * heads // shards
    vmem = pl.BlockSpec(memory_space=pltpu.VMEM)
    dma = pltpu.SemaphoreType.DMA
    return pl.pallas_call(
        functools.partial(move_kernel, sections, shards),
        out_shape=(
            jax.ShapeDtypeStruct((heads, piece, shards * width), jnp.bfloat16),
            jax.ShapeDtypeStruct((row_block, 2 * HD), jnp.bfloat16),
        ),
        in_specs=[pl.BlockSpec(memory_space=pltpu.SMEM), vmem, vmem],
        out_specs=(pl.BlockSpec(memory_space=pl.ANY), vmem),
        scratch_shapes=[pltpu.VMEM((sections, piece, width), jnp.bfloat16)] * shards + [
            pltpu.VMEM((shards, sections, piece, width), jnp.bfloat16),
            pltpu.VMEM((shards, heads, piece, width), jnp.bfloat16),
            pltpu.VMEM((shards, rows_in, width), jnp.bfloat16),
            pltpu.VMEM((heads, 2 * HD, ROWS), jnp.float32),
            pltpu.VMEM((shards, row_block, 2 * HD), jnp.float32),
            pltpu.VMEM((shards, row_block, 2 * HD), jnp.float32),
            dma((shards, sections)), dma((shards, sections)),
            dma((shards, sections)), dma((shards, sections)),
            dma((shards,)), dma((shards,)), dma((shards,)), dma((shards,)), dma((shards,)), dma((shards,)),
            dma(()),
        ],
        compiler_params=pltpu.CompilerParams(
            collective_id=0, has_side_effects=True, vmem_limit_bytes=40 * 2**20),
        cost_estimate=pl.CostEstimate(flops=2 * ROWS * width * heads * piece * shards, bytes_accessed=4 * weights.size, transcendentals=0),
    )(source, weights, hidden)


def attend_kernel(query_ref, cache_ref, fresh_ref, length_ref, out_ref):
    scale = 1.0 / math.sqrt(HD)
    query = query_ref[...]
    cache = cache_ref[...]
    fresh = fresh_ref[...].astype(jnp.float32)
    scores = lax.dot_general(query, cache[:, :, :HD], (((2,), (2,)), ((0,), (0,))),
                             preferred_element_type=jnp.float32) * scale
    slot = lax.broadcasted_iota(jnp.int32, scores.shape, 2)
    valid = slot < length_ref[...]
    scores = jnp.where(valid, scores, -1e30)
    fresh_score = jnp.sum(query.astype(jnp.float32) * fresh[:, :, :HD], axis=-1, keepdims=True) * scale
    highest = jnp.maximum(jnp.max(scores, axis=-1, keepdims=True), fresh_score)
    weights = jnp.where(valid, jnp.exp(scores - highest), 0.0)
    fresh_weight = jnp.exp(fresh_score - highest)
    total = jnp.sum(weights, axis=-1, keepdims=True) + fresh_weight
    probs = (weights / total).astype(jnp.bfloat16)
    fresh_prob = (fresh_weight / total).astype(jnp.bfloat16).astype(jnp.float32)
    context = lax.dot_general(probs, cache[:, :, HD:], (((2,), (1,)), ((0,), (0,))),
                              preferred_element_type=jnp.float32)
    context = context + fresh_prob * fresh[:, :, HD:]
    out_ref[...] = context.astype(out_ref.dtype)


def attend_rows(queries, cache, fresh, row_lengths):
    entries = cache.shape[0]
    step = 8
    spec = lambda *tail: pl.BlockSpec((step,) + tail, lambda i: (i, 0, 0))
    lengths = jnp.broadcast_to(row_lengths[:, None, None], (entries, 1, LEN))
    return pl.pallas_call(
        attend_kernel,
        grid=(entries // step,),
        out_shape=jax.ShapeDtypeStruct((entries, QPK, HD), jnp.bfloat16),
        in_specs=[spec(QPK, HD), spec(LEN, 2 * HD), spec(1, 2 * HD), spec(1, LEN)],
        out_specs=spec(QPK, HD),
    )(queries.reshape(entries, QPK, HD), cache, fresh.reshape(entries, 1, 2 * HD), lengths).reshape(entries, QPK * HD)


def chunk_body(train_weights, section_to_group, hidden, queries, kv_cache, lengths):
    shards = lax.axis_size("shard")
    per_head = shards // KVH
    row_block = ROWS // per_head
    piece = 2 * HD // shards
    source = jnp.argsort(section_to_group).astype(jnp.int32)
    flipped = train_weights[0].astype(jnp.bfloat16).T
    weights = flipped.reshape(KVH, shards, piece, flipped.shape[1])
    kept, fresh = move(weights, hidden, source)
    block = lax.axis_index("shard") % per_head
    row_lengths = lax.dynamic_slice_in_dim(lengths, block * row_block, row_block, 0)
    context = attend_rows(queries, kv_cache, fresh, row_lengths)
    return (context, kept[None])


def solution(mesh):
    sections, shards = mesh.shape["section"], mesh.shape["shard"]
    chunked = (
        sections == KVH and shards % KVH == 0 and shards & (shards - 1) == 0
        and (2 * HD // shards) % 16 == 0 and (ROWS // shards) % 16 == 0
    )
    body = chunk_body if chunked else plain_body
    return jax.shard_map(
        body,
        mesh=mesh,
        in_specs=(
            P("section", "shard", None),
            P(),
            P(("section", "shard"), None),
            P(("section", "shard"), None),
            P(("section", "shard"), None, None),
            P("section"),
        ),
        out_specs=(P(("section", "shard"), None), P("section", None, "shard", None)),
        check_vma=False,
    )
```

```python
import functools
import math

import jax
import jax.numpy as jnp
from jax import lax
from jax.experimental import pallas as pl
from jax.experimental.pallas import tpu as pltpu
from jax.sharding import PartitionSpec as P

D = 16384
HD = 128
QPK = 16
KVH = 4
LEN = 128
ROWS = 128


def route(blocks, source):
    spread = lax.all_to_all(blocks, "section", split_axis=2, concat_axis=0, tiled=True)
    picked = jnp.take(spread, source, axis=0)
    return lax.all_to_all(picked, "section", split_axis=0, concat_axis=2, tiled=True)


def attend(query_rows, cache_rows, fresh_rows, row_lengths):
    score_scale = 1.0 / math.sqrt(HD)
    cached_keys = cache_rows[:, :, :HD]
    cached_values = cache_rows[:, :, HD:]
    key_new = fresh_rows[:, :HD]
    value_new = fresh_rows[:, HD:]
    scores = (
        jnp.einsum("rhd,rtd->rht", query_rows, cached_keys, preferred_element_type=jnp.float32)
        * score_scale
    )
    valid = jnp.arange(LEN)[None, None, :] < row_lengths[:, None, None]
    scores = jnp.where(valid, scores, -1e30)
    fresh_score = (
        jnp.einsum("rhd,rd->rh", query_rows, key_new, preferred_element_type=jnp.float32)
        * score_scale
    )
    highest = jnp.maximum(jnp.max(scores, axis=-1), fresh_score)
    weights = jnp.where(valid, jnp.exp(scores - highest[..., None]), 0.0)
    fresh_weight = jnp.exp(fresh_score - highest)
    total = jnp.sum(weights, axis=-1) + fresh_weight
    probs = (weights / total[..., None]).astype(jnp.bfloat16)
    fresh_prob = (fresh_weight / total).astype(jnp.bfloat16)
    context = jnp.einsum("rht,rtd->rhd", probs, cached_values, preferred_element_type=jnp.float32)
    context = (
        context
        + fresh_prob.astype(jnp.float32)[..., None] * value_new.astype(jnp.float32)[:, None, :]
    )
    return context.reshape(context.shape[0], QPK * HD).astype(jnp.bfloat16)


def plain_body(train_weights, section_to_group, hidden, queries, kv_cache, lengths):
    shards = lax.axis_size("shard")
    per_head = shards // KVH
    row_block = ROWS // per_head
    piece_cols = 2 * HD // shards
    source = jnp.argsort(section_to_group)
    flipped = train_weights[0].astype(jnp.bfloat16).T
    slice_rows = flipped.shape[1]
    routed = route(flipped[None], source)[0]
    pieces = routed.reshape(KVH, shards, piece_cols, slice_rows).transpose(1, 0, 2, 3)
    column_block = lax.all_to_all(pieces, "shard", split_axis=0, concat_axis=3, tiled=True)
    column_block = column_block.reshape(KVH * piece_cols, D)
    feature_block = lax.all_to_all(hidden, "shard", split_axis=1, concat_axis=0, tiled=True)
    partial_value = lax.dot_general(
        feature_block, routed, (((1,), (1,)), ((), ())), preferred_element_type=jnp.float32
    )
    arranged = partial_value.reshape(per_head, row_block, KVH, 2 * HD).transpose(2, 0, 1, 3)
    arranged = arranged.reshape(shards * row_block, 2 * HD)
    fresh = lax.psum_scatter(arranged, "shard", scatter_dimension=0, tiled=True).astype(
        jnp.bfloat16
    )
    position = lax.axis_index("shard")
    block_index = position % per_head
    row_lengths = lax.dynamic_slice_in_dim(lengths, block_index * row_block, row_block, 0)
    query_rows = queries.reshape(row_block, QPK, HD)
    context = attend(query_rows, kv_cache, fresh, row_lengths)
    layer_out = column_block.reshape(1, KVH, piece_cols, D)
    return (context, layer_out)


def flip(index, mask, size):
    result, bit = 0, 1
    while bit < size:
        value = (index // bit) % 2
        if mask & bit:
            value = 1 - value
        result = result + value * bit
        bit *= 2
    return result


def move_kernel(sections, shards, source_ref, train_ref, hidden_ref, out_ref, fresh_ref, *scratch):
    spread = scratch[:shards]
    (stage, picked, feat, part, part_send, part_recv,
     a_send, a_recv, b_send, b_recv, c_send, c_recv, h_send, h_recv, p_send, p_recv, local, w_ref, raw, raw_sem) = scratch[shards:]
    me = lax.axis_index("section")
    pos = lax.axis_index("shard")
    heads, _, piece, width = w_ref.shape
    rows_in = hidden_ref.shape[0]
    per_head = shards // heads
    row_block = ROWS // per_head

    lanes = raw.shape[-1]
    together = lanes // piece
    groups = shards // together

    def group_of(i):
        return flip(pos // together, groups - 1 - i, groups)

    def load_copy(i, h):
        start = pl.multiple_of((h * groups + group_of(i)) * lanes, lanes)
        return pltpu.make_async_copy(train_ref.at[:, pl.ds(start, lanes)], raw.at[i, h], raw_sem.at[i, h])

    def turn(i, h):
        load_copy(i, h).wait()
        block = raw[i, h].astype(jnp.bfloat16).T
        w_ref[h, pl.ds(group_of(i) * together, together)] = block.reshape(together, piece, width)

    for i in range(groups):
        for h in range(heads):
            load_copy(i, h).start()

    barrier = pltpu.get_barrier_semaphore()
    for j in range(1, sections):
        pl.semaphore_signal(barrier, inc=1, device_id={"section": flip(me, j, sections)}, device_id_type=pl.DeviceIdType.MESH)
    for j in range(1, shards):
        pl.semaphore_signal(barrier, inc=1, device_id={"shard": flip(pos, j, shards)}, device_id_type=pl.DeviceIdType.MESH)
    pl.semaphore_wait(barrier, sections + shards - 2)

    def remote(src, dst, send, recv, **target):
        return pltpu.make_async_remote_copy(
            src_ref=src, dst_ref=dst, send_sem=send, recv_sem=recv,
            device_id=target, device_id_type=pl.DeviceIdType.MESH)

    masks = list(range(shards - 1, -1, -1))

    def spread_copies(k):
        p = flip(pos, masks[k], shards)
        copies = []
        for j in range(1, sections):
            t = flip(me, j, sections)
            copies.append(remote(w_ref.at[t, p], spread[k].at[me], a_send.at[k, j], a_recv.at[k, j], section=t))
        return copies

    def collect_copies(k):
        copies = []
        for j in range(1, sections):
            t = flip(me, j, sections)
            copies.append(remote(stage.at[k, t], picked.at[k, me], b_send.at[k, j], b_recv.at[k, j], section=t))
        return copies

    columns = pl.ds(pl.multiple_of(pos * width, width), width)

    def keep_copy(k):
        p = flip(pos, masks[k], shards)
        if masks[k] == 0:
            return pltpu.make_async_copy(picked.at[k], out_ref.at[:, :, columns], local)
        return remote(picked.at[k], out_ref.at[:, :, columns], c_send.at[k], c_recv.at[k], shard=p)

    def hidden_copy(j):
        p = flip(pos, j, shards)
        return remote(hidden_ref.at[:, pl.ds(pl.multiple_of(p * width, width), width)], feat.at[pos],
                      h_send.at[j], h_recv.at[j], shard=p)

    def start_spread(k):
        for copy in spread_copies(k):
            copy.start()
        spread[k][me] = w_ref[me, flip(pos, masks[k], shards)]

    ahead = AHEAD
    for j in range(shards - 1, 0, -1):
        hidden_copy(j).start()
    for h in range(heads):
        turn(0, h)
    for k in range(min(ahead, shards)):
        start_spread(k)
    feat[pos] = hidden_ref[:, columns]

    def collect(k):
        for copy in spread_copies(k):
            copy.wait()
        for g in range(sections):
            stage[k, g] = spread[k][source_ref[g]]
        picked[k, me] = stage[k, me]
        for copy in collect_copies(k):
            copy.start()

    def forward(k):
        for copy in collect_copies(k):
            copy.wait()
        keep_copy(k).start()
        if k == 0:
            for j in range(1, shards):
                hidden_copy(j).wait()
        p = flip(pos, masks[k], shards)
        value = lax.dot_general(
            picked[k].reshape(heads * piece, width), feat[...].reshape(shards * rows_in, width),
            (((1,), (1,)), ((), ())), preferred_element_type=jnp.float32)
        for h in range(heads):
            part[h, pl.ds(pl.multiple_of(p * piece, piece), piece), :] = value[h * piece:(h + 1) * piece]

    for k in range(shards):
        collect(k)
        if k + ahead < shards:
            start_spread(k + ahead)
        if k < groups - 1:
            for h in range(heads):
                turn(k + 1, h)
        if k >= 1:
            forward(k - 1)
    forward(shards - 1)

    for h in range(heads):
        turned = part[h].T
        for b in range(per_head):
            part_send[h * per_head + b] = turned[b * row_block:(b + 1) * row_block]

    def part_copy(j):
        p = flip(pos, j, shards)
        return remote(part_send.at[p], part_recv.at[j], p_send.at[j], p_recv.at[j], shard=p)

    for j in range(shards - 1, 0, -1):
        part_copy(j).start()
    total = part_send[pos]
    for j in range(1, shards):
        part_copy(j).wait()
        total = total + part_recv[j]
    fresh_ref[...] = total.astype(fresh_ref.dtype)
    for k in range(shards):
        keep_copy(k).wait()


AHEAD = 1
LANES = 128


def move(weights, hidden, source):
    sections, shards = lax.axis_size("section"), lax.axis_size("shard")
    heads, piece, width = KVH, 2 * HD // shards, weights.shape[0]
    rows_in = hidden.shape[0]
    row_block = ROWS * heads // shards
    vmem = pl.BlockSpec(memory_space=pltpu.VMEM)
    dma = pltpu.SemaphoreType.DMA
    return pl.pallas_call(
        functools.partial(move_kernel, sections, shards),
        out_shape=(
            jax.ShapeDtypeStruct((heads, piece, shards * width), jnp.bfloat16),
            jax.ShapeDtypeStruct((row_block, 2 * HD), jnp.bfloat16),
        ),
        in_specs=[pl.BlockSpec(memory_space=pltpu.SMEM), pl.BlockSpec(memory_space=pl.ANY), vmem],
        out_specs=(pl.BlockSpec(memory_space=pl.ANY), vmem),
        scratch_shapes=[pltpu.VMEM((sections, piece, width), jnp.bfloat16)] * shards + [
            pltpu.VMEM((shards, sections, piece, width), jnp.bfloat16),
            pltpu.VMEM((shards, heads, piece, width), jnp.bfloat16),
            pltpu.VMEM((shards, rows_in, width), jnp.bfloat16),
            pltpu.VMEM((heads, 2 * HD, ROWS), jnp.float32),
            pltpu.VMEM((shards, row_block, 2 * HD), jnp.float32),
            pltpu.VMEM((shards, row_block, 2 * HD), jnp.float32),
            dma((shards, sections)), dma((shards, sections)),
            dma((shards, sections)), dma((shards, sections)),
            dma((shards,)), dma((shards,)), dma((shards,)), dma((shards,)), dma((shards,)), dma((shards,)),
            dma(()),
            pltpu.VMEM((heads, shards, piece, width), jnp.bfloat16),
            pltpu.VMEM((shards * piece // LANES, heads, width, LANES), jnp.float32),
            dma((shards * piece // LANES, heads)),
        ],
        compiler_params=pltpu.CompilerParams(
            collective_id=0, has_side_effects=True, vmem_limit_bytes=40 * 2**20),
        cost_estimate=pl.CostEstimate(flops=2 * ROWS * width * heads * piece * shards, bytes_accessed=4 * weights.size, transcendentals=0),
    )(source, weights, hidden)


def attend_kernel(query_ref, cache_ref, fresh_ref, length_ref, out_ref):
    scale = 1.0 / math.sqrt(HD)
    query = query_ref[...]
    cache = cache_ref[...]
    fresh = fresh_ref[...].astype(jnp.float32)
    scores = lax.dot_general(query, cache[:, :, :HD], (((2,), (2,)), ((0,), (0,))),
                             preferred_element_type=jnp.float32) * scale
    slot = lax.broadcasted_iota(jnp.int32, scores.shape, 2)
    valid = slot < length_ref[...]
    scores = jnp.where(valid, scores, -1e30)
    fresh_score = jnp.sum(query.astype(jnp.float32) * fresh[:, :, :HD], axis=-1, keepdims=True) * scale
    highest = jnp.maximum(jnp.max(scores, axis=-1, keepdims=True), fresh_score)
    weights = jnp.where(valid, jnp.exp(scores - highest), 0.0)
    fresh_weight = jnp.exp(fresh_score - highest)
    total = jnp.sum(weights, axis=-1, keepdims=True) + fresh_weight
    probs = (weights / total).astype(jnp.bfloat16)
    fresh_prob = (fresh_weight / total).astype(jnp.bfloat16).astype(jnp.float32)
    context = lax.dot_general(probs, cache[:, :, HD:], (((2,), (1,)), ((0,), (0,))),
                              preferred_element_type=jnp.float32)
    context = context + fresh_prob * fresh[:, :, HD:]
    out_ref[...] = context.astype(out_ref.dtype)


def attend_rows(queries, cache, fresh, row_lengths):
    entries = cache.shape[0]
    step = 8
    spec = lambda *tail: pl.BlockSpec((step,) + tail, lambda i: (i, 0, 0))
    lengths = jnp.broadcast_to(row_lengths[:, None, None], (entries, 1, LEN))
    return pl.pallas_call(
        attend_kernel,
        grid=(entries // step,),
        out_shape=jax.ShapeDtypeStruct((entries, QPK, HD), jnp.bfloat16),
        in_specs=[spec(QPK, HD), spec(LEN, 2 * HD), spec(1, 2 * HD), spec(1, LEN)],
        out_specs=spec(QPK, HD),
    )(queries.reshape(entries, QPK, HD), cache, fresh.reshape(entries, 1, 2 * HD), lengths).reshape(entries, QPK * HD)


def chunk_body(train_weights, section_to_group, hidden, queries, kv_cache, lengths):
    shards = lax.axis_size("shard")
    per_head = shards // KVH
    row_block = ROWS // per_head
    source = jnp.argsort(section_to_group).astype(jnp.int32)
    kept, fresh = move(train_weights[0], hidden, source)
    block = lax.axis_index("shard") % per_head
    row_lengths = lax.dynamic_slice_in_dim(lengths, block * row_block, row_block, 0)
    context = attend_rows(queries, kv_cache, fresh, row_lengths)
    return (context, kept[None])


def solution(mesh):
    sections, shards = mesh.shape["section"], mesh.shape["shard"]
    chunked = (
        sections == KVH and shards % KVH == 0 and shards & (shards - 1) == 0
        and (2 * HD // shards) % 16 == 0 and LANES % (2 * HD // shards) == 0 and (ROWS // shards) % 16 == 0
    )
    body = chunk_body if chunked else plain_body
    return jax.shard_map(
        body,
        mesh=mesh,
        in_specs=(
            P("section", "shard", None),
            P(),
            P(("section", "shard"), None),
            P(("section", "shard"), None),
            P(("section", "shard"), None, None),
            P("section"),
        ),
        out_specs=(P(("section", "shard"), None), P("section", None, "shard", None)),
        check_vma=False,
    )
```

```python
import functools
import math

import jax
import jax.numpy as jnp
from jax import lax
from jax.experimental import pallas as pl
from jax.experimental.pallas import tpu as pltpu
from jax.sharding import PartitionSpec as P

D = 16384
HD = 128
QPK = 16
KVH = 4
LEN = 128
ROWS = 128


def route(blocks, source):
    spread = lax.all_to_all(blocks, "section", split_axis=2, concat_axis=0, tiled=True)
    picked = jnp.take(spread, source, axis=0)
    return lax.all_to_all(picked, "section", split_axis=0, concat_axis=2, tiled=True)


def attend(query_rows, cache_rows, fresh_rows, row_lengths):
    score_scale = 1.0 / math.sqrt(HD)
    cached_keys = cache_rows[:, :, :HD]
    cached_values = cache_rows[:, :, HD:]
    key_new = fresh_rows[:, :HD]
    value_new = fresh_rows[:, HD:]
    scores = (
        jnp.einsum("rhd,rtd->rht", query_rows, cached_keys, preferred_element_type=jnp.float32)
        * score_scale
    )
    valid = jnp.arange(LEN)[None, None, :] < row_lengths[:, None, None]
    scores = jnp.where(valid, scores, -1e30)
    fresh_score = (
        jnp.einsum("rhd,rd->rh", query_rows, key_new, preferred_element_type=jnp.float32)
        * score_scale
    )
    highest = jnp.maximum(jnp.max(scores, axis=-1), fresh_score)
    weights = jnp.where(valid, jnp.exp(scores - highest[..., None]), 0.0)
    fresh_weight = jnp.exp(fresh_score - highest)
    total = jnp.sum(weights, axis=-1) + fresh_weight
    probs = (weights / total[..., None]).astype(jnp.bfloat16)
    fresh_prob = (fresh_weight / total).astype(jnp.bfloat16)
    context = jnp.einsum("rht,rtd->rhd", probs, cached_values, preferred_element_type=jnp.float32)
    context = (
        context
        + fresh_prob.astype(jnp.float32)[..., None] * value_new.astype(jnp.float32)[:, None, :]
    )
    return context.reshape(context.shape[0], QPK * HD).astype(jnp.bfloat16)


def plain_body(train_weights, section_to_group, hidden, queries, kv_cache, lengths):
    shards = lax.axis_size("shard")
    per_head = shards // KVH
    row_block = ROWS // per_head
    piece_cols = 2 * HD // shards
    source = jnp.argsort(section_to_group)
    flipped = train_weights[0].astype(jnp.bfloat16).T
    slice_rows = flipped.shape[1]
    routed = route(flipped[None], source)[0]
    pieces = routed.reshape(KVH, shards, piece_cols, slice_rows).transpose(1, 0, 2, 3)
    column_block = lax.all_to_all(pieces, "shard", split_axis=0, concat_axis=3, tiled=True)
    column_block = column_block.reshape(KVH * piece_cols, D)
    feature_block = lax.all_to_all(hidden, "shard", split_axis=1, concat_axis=0, tiled=True)
    partial_value = lax.dot_general(
        feature_block, routed, (((1,), (1,)), ((), ())), preferred_element_type=jnp.float32
    )
    arranged = partial_value.reshape(per_head, row_block, KVH, 2 * HD).transpose(2, 0, 1, 3)
    arranged = arranged.reshape(shards * row_block, 2 * HD)
    fresh = lax.psum_scatter(arranged, "shard", scatter_dimension=0, tiled=True).astype(
        jnp.bfloat16
    )
    position = lax.axis_index("shard")
    block_index = position % per_head
    row_lengths = lax.dynamic_slice_in_dim(lengths, block_index * row_block, row_block, 0)
    query_rows = queries.reshape(row_block, QPK, HD)
    context = attend(query_rows, kv_cache, fresh, row_lengths)
    layer_out = column_block.reshape(1, KVH, piece_cols, D)
    return (context, layer_out)


def flip(index, mask, size):
    result, bit = 0, 1
    while bit < size:
        value = (index // bit) % 2
        if mask & bit:
            value = 1 - value
        result = result + value * bit
        bit *= 2
    return result


def move_kernel(sections, shards, source_ref, train_ref, hidden_ref, query_ref, cache_ref, length_ref, out_ref, context_ref, *scratch):
    spread = scratch[:shards]
    (stage, picked, feat, part, part_send, part_recv,
     a_send, a_recv, b_send, b_recv, c_send, c_recv, h_send, h_recv, p_send, p_recv, local, w_ref, raw, raw_sem, held, held_max, held_sum) = scratch[shards:]
    me = lax.axis_index("section")
    pos = lax.axis_index("shard")
    heads, _, piece, width = w_ref.shape
    rows_in = hidden_ref.shape[0]
    per_head = shards // heads
    row_block = ROWS // per_head

    lanes = raw.shape[-1]
    together = lanes // piece
    groups = shards // together

    def group_of(i):
        return flip(pos // together, groups - 1 - i, groups)

    def load_copy(i, h):
        start = pl.multiple_of((h * groups + group_of(i)) * lanes, lanes)
        return pltpu.make_async_copy(train_ref.at[:, pl.ds(start, lanes)], raw.at[i, h], raw_sem.at[i, h])

    def turn(i, h):
        load_copy(i, h).wait()
        block = raw[i, h].astype(jnp.bfloat16).T
        w_ref[h, pl.ds(group_of(i) * together, together)] = block.reshape(together, piece, width)

    for i in range(groups):
        for h in range(heads):
            load_copy(i, h).start()

    barrier = pltpu.get_barrier_semaphore()
    for j in range(1, sections):
        pl.semaphore_signal(barrier, inc=1, device_id={"section": flip(me, j, sections)}, device_id_type=pl.DeviceIdType.MESH)
    for j in range(1, shards):
        pl.semaphore_signal(barrier, inc=1, device_id={"shard": flip(pos, j, shards)}, device_id_type=pl.DeviceIdType.MESH)
    pl.semaphore_wait(barrier, sections + shards - 2)

    def remote(src, dst, send, recv, **target):
        return pltpu.make_async_remote_copy(
            src_ref=src, dst_ref=dst, send_sem=send, recv_sem=recv,
            device_id=target, device_id_type=pl.DeviceIdType.MESH)

    masks = list(range(shards - 1, -1, -1))

    def spread_copies(k):
        p = flip(pos, masks[k], shards)
        copies = []
        for j in range(1, sections):
            t = flip(me, j, sections)
            copies.append(remote(w_ref.at[t, p], spread[k].at[me], a_send.at[k, j], a_recv.at[k, j], section=t))
        return copies

    def collect_copies(k):
        copies = []
        for j in range(1, sections):
            t = flip(me, j, sections)
            copies.append(remote(stage.at[k, t], picked.at[k, me], b_send.at[k, j], b_recv.at[k, j], section=t))
        return copies

    columns = pl.ds(pl.multiple_of(pos * width, width), width)

    def keep_copy(k):
        p = flip(pos, masks[k], shards)
        if masks[k] == 0:
            return pltpu.make_async_copy(picked.at[k], out_ref.at[:, :, columns], local)
        return remote(picked.at[k], out_ref.at[:, :, columns], c_send.at[k], c_recv.at[k], shard=p)

    def hidden_copy(j):
        p = flip(pos, j, shards)
        return remote(hidden_ref.at[:, pl.ds(pl.multiple_of(p * width, width), width)], feat.at[pos],
                      h_send.at[j], h_recv.at[j], shard=p)

    def start_spread(k):
        for copy in spread_copies(k):
            copy.start()
        spread[k][me] = w_ref[me, flip(pos, masks[k], shards)]

    ahead = AHEAD
    for j in range(shards - 1, 0, -1):
        hidden_copy(j).start()
    for h in range(heads):
        turn(0, h)
    for k in range(min(ahead, shards)):
        start_spread(k)
    feat[pos] = hidden_ref[:, columns]

    def collect(k):
        for copy in spread_copies(k):
            copy.wait()
        for g in range(sections):
            stage[k, g] = spread[k][source_ref[g]]
        picked[k, me] = stage[k, me]
        for copy in collect_copies(k):
            copy.start()

    def forward(k):
        for copy in collect_copies(k):
            copy.wait()
        keep_copy(k).start()
        if k == 0:
            for j in range(1, shards):
                hidden_copy(j).wait()
        p = flip(pos, masks[k], shards)
        value = lax.dot_general(
            picked[k].reshape(heads * piece, width), feat[...].reshape(shards * rows_in, width),
            (((1,), (1,)), ((), ())), preferred_element_type=jnp.float32)
        for h in range(heads):
            part[h, pl.ds(pl.multiple_of(p * piece, piece), piece), :] = value[h * piece:(h + 1) * piece]

    scale = 1.0 / math.sqrt(HD)
    some = cache_ref.shape[0] // shards

    def attend_cached(k):
        rows = slice(k * some, (k + 1) * some)
        cache = cache_ref[rows]
        scores = lax.dot_general(query_ref[rows], cache[:, :, :HD], (((2,), (2,)), ((0,), (0,))),
                                 preferred_element_type=jnp.float32) * scale
        valid = lax.broadcasted_iota(jnp.int32, scores.shape, 2) < length_ref[rows]
        scores = jnp.where(valid, scores, -1e30)
        highest = jnp.max(scores, axis=-1, keepdims=True)
        weights = jnp.where(valid, jnp.exp(scores - highest), 0.0)
        held[rows] = lax.dot_general(weights.astype(jnp.bfloat16), cache[:, :, HD:], (((2,), (1,)), ((0,), (0,))),
                                     preferred_element_type=jnp.float32)
        held_max[rows] = jnp.broadcast_to(highest, scores.shape)
        held_sum[rows] = jnp.broadcast_to(jnp.sum(weights, axis=-1, keepdims=True), scores.shape)

    def attend_fresh(k, fresh):
        rows = slice(k * some, (k + 1) * some)
        key, value = fresh[rows, :HD][:, None, :], fresh[rows, HD:][:, None, :]
        score = jnp.sum(query_ref[rows].astype(jnp.float32) * key, axis=-1, keepdims=True) * scale
        highest = jnp.maximum(held_max[rows], score)
        old = jnp.exp(held_max[rows] - highest)
        new = jnp.exp(score - highest)
        total = held_sum[rows] * old + new
        prob = (new / total).astype(jnp.bfloat16).astype(jnp.float32)
        context_ref[rows] = (held[rows] * (old / total) + prob * value).astype(context_ref.dtype)

    for k in range(shards):
        collect(k)
        if k + ahead < shards:
            start_spread(k + ahead)
        if k < groups - 1:
            for h in range(heads):
                turn(k + 1, h)
        if k >= 1:
            forward(k - 1)
        attend_cached(k)
    forward(shards - 1)

    for h in range(heads):
        turned = part[h].T
        for b in range(per_head):
            part_send[h * per_head + b] = turned[b * row_block:(b + 1) * row_block]

    def part_copy(j):
        p = flip(pos, j, shards)
        return remote(part_send.at[p], part_recv.at[j], p_send.at[j], p_recv.at[j], shard=p)

    for j in range(shards - 1, 0, -1):
        part_copy(j).start()
    total = part_send[pos]
    for j in range(1, shards):
        part_copy(j).wait()
        total = total + part_recv[j]
    fresh = total.astype(jnp.bfloat16).astype(jnp.float32)
    for k in range(shards):
        attend_fresh(k, fresh)
    for k in range(shards):
        keep_copy(k).wait()


AHEAD = 1
LANES = 128


def move(weights, hidden, source, queries, cache, row_lengths):
    sections, shards = lax.axis_size("section"), lax.axis_size("shard")
    heads, piece, width = KVH, 2 * HD // shards, weights.shape[0]
    rows_in = hidden.shape[0]
    row_block = ROWS * heads // shards
    entries = cache.shape[0]
    lengths = jnp.broadcast_to(row_lengths[:, None, None], (entries, 1, LEN))
    vmem = pl.BlockSpec(memory_space=pltpu.VMEM)
    dma = pltpu.SemaphoreType.DMA
    return pl.pallas_call(
        functools.partial(move_kernel, sections, shards),
        out_shape=(
            jax.ShapeDtypeStruct((heads, piece, shards * width), jnp.bfloat16),
            jax.ShapeDtypeStruct((entries, QPK, HD), jnp.bfloat16),
        ),
        in_specs=[pl.BlockSpec(memory_space=pltpu.SMEM), pl.BlockSpec(memory_space=pl.ANY), vmem, vmem, vmem, vmem],
        out_specs=(pl.BlockSpec(memory_space=pl.ANY), vmem),
        scratch_shapes=[pltpu.VMEM((sections, piece, width), jnp.bfloat16)] * shards + [
            pltpu.VMEM((shards, sections, piece, width), jnp.bfloat16),
            pltpu.VMEM((shards, heads, piece, width), jnp.bfloat16),
            pltpu.VMEM((shards, rows_in, width), jnp.bfloat16),
            pltpu.VMEM((heads, 2 * HD, ROWS), jnp.float32),
            pltpu.VMEM((shards, row_block, 2 * HD), jnp.float32),
            pltpu.VMEM((shards, row_block, 2 * HD), jnp.float32),
            dma((shards, sections)), dma((shards, sections)),
            dma((shards, sections)), dma((shards, sections)),
            dma((shards,)), dma((shards,)), dma((shards,)), dma((shards,)), dma((shards,)), dma((shards,)),
            dma(()),
            pltpu.VMEM((heads, shards, piece, width), jnp.bfloat16),
            pltpu.VMEM((shards * piece // LANES, heads, width, LANES), jnp.float32),
            dma((shards * piece // LANES, heads)),
        ] + [pltpu.VMEM((entries, QPK, HD), jnp.float32)] * 3,
        compiler_params=pltpu.CompilerParams(
            collective_id=0, has_side_effects=True, vmem_limit_bytes=50 * 2**20),
        cost_estimate=pl.CostEstimate(flops=2 * ROWS * width * heads * piece * shards, bytes_accessed=4 * weights.size, transcendentals=0),
    )(source, weights, hidden, queries.reshape(entries, QPK, HD), cache, lengths)


def chunk_body(train_weights, section_to_group, hidden, queries, kv_cache, lengths):
    shards = lax.axis_size("shard")
    per_head = shards // KVH
    row_block = ROWS // per_head
    source = jnp.argsort(section_to_group).astype(jnp.int32)
    block = lax.axis_index("shard") % per_head
    row_lengths = lax.dynamic_slice_in_dim(lengths, block * row_block, row_block, 0)
    kept, context = move(train_weights[0], hidden, source, queries, kv_cache, row_lengths)
    context = context.reshape(queries.shape)
    return (context, kept[None])


def solution(mesh):
    sections, shards = mesh.shape["section"], mesh.shape["shard"]
    chunked = (
        sections == KVH and shards % KVH == 0 and shards & (shards - 1) == 0
        and (2 * HD // shards) % 16 == 0 and LANES % (2 * HD // shards) == 0 and (ROWS // shards) % 16 == 0
    )
    body = chunk_body if chunked else plain_body
    return jax.shard_map(
        body,
        mesh=mesh,
        in_specs=(
            P("section", "shard", None),
            P(),
            P(("section", "shard"), None),
            P(("section", "shard"), None),
            P(("section", "shard"), None, None),
            P("section"),
        ),
        out_specs=(P(("section", "shard"), None), P("section", None, "shard", None)),
        check_vma=False,
    )
```

```python
import functools
import math

import jax
import jax.numpy as jnp
from jax import lax
from jax.experimental import pallas as pl
from jax.experimental.pallas import tpu as pltpu
from jax.sharding import PartitionSpec as P

D = 16384
HD = 128
QPK = 16
KVH = 4
LEN = 128
ROWS = 128


def route(blocks, source):
    spread = lax.all_to_all(blocks, "section", split_axis=2, concat_axis=0, tiled=True)
    picked = jnp.take(spread, source, axis=0)
    return lax.all_to_all(picked, "section", split_axis=0, concat_axis=2, tiled=True)


def attend(query_rows, cache_rows, fresh_rows, row_lengths):
    score_scale = 1.0 / math.sqrt(HD)
    cached_keys = cache_rows[:, :, :HD]
    cached_values = cache_rows[:, :, HD:]
    key_new = fresh_rows[:, :HD]
    value_new = fresh_rows[:, HD:]
    scores = (
        jnp.einsum("rhd,rtd->rht", query_rows, cached_keys, preferred_element_type=jnp.float32)
        * score_scale
    )
    valid = jnp.arange(LEN)[None, None, :] < row_lengths[:, None, None]
    scores = jnp.where(valid, scores, -1e30)
    fresh_score = (
        jnp.einsum("rhd,rd->rh", query_rows, key_new, preferred_element_type=jnp.float32)
        * score_scale
    )
    highest = jnp.maximum(jnp.max(scores, axis=-1), fresh_score)
    weights = jnp.where(valid, jnp.exp(scores - highest[..., None]), 0.0)
    fresh_weight = jnp.exp(fresh_score - highest)
    total = jnp.sum(weights, axis=-1) + fresh_weight
    probs = (weights / total[..., None]).astype(jnp.bfloat16)
    fresh_prob = (fresh_weight / total).astype(jnp.bfloat16)
    context = jnp.einsum("rht,rtd->rhd", probs, cached_values, preferred_element_type=jnp.float32)
    context = (
        context
        + fresh_prob.astype(jnp.float32)[..., None] * value_new.astype(jnp.float32)[:, None, :]
    )
    return context.reshape(context.shape[0], QPK * HD).astype(jnp.bfloat16)


def plain_body(train_weights, section_to_group, hidden, queries, kv_cache, lengths):
    shards = lax.axis_size("shard")
    per_head = shards // KVH
    row_block = ROWS // per_head
    piece_cols = 2 * HD // shards
    source = jnp.argsort(section_to_group)
    flipped = train_weights[0].astype(jnp.bfloat16).T
    slice_rows = flipped.shape[1]
    routed = route(flipped[None], source)[0]
    pieces = routed.reshape(KVH, shards, piece_cols, slice_rows).transpose(1, 0, 2, 3)
    column_block = lax.all_to_all(pieces, "shard", split_axis=0, concat_axis=3, tiled=True)
    column_block = column_block.reshape(KVH * piece_cols, D)
    feature_block = lax.all_to_all(hidden, "shard", split_axis=1, concat_axis=0, tiled=True)
    partial_value = lax.dot_general(
        feature_block, routed, (((1,), (1,)), ((), ())), preferred_element_type=jnp.float32
    )
    arranged = partial_value.reshape(per_head, row_block, KVH, 2 * HD).transpose(2, 0, 1, 3)
    arranged = arranged.reshape(shards * row_block, 2 * HD)
    fresh = lax.psum_scatter(arranged, "shard", scatter_dimension=0, tiled=True).astype(
        jnp.bfloat16
    )
    position = lax.axis_index("shard")
    block_index = position % per_head
    row_lengths = lax.dynamic_slice_in_dim(lengths, block_index * row_block, row_block, 0)
    query_rows = queries.reshape(row_block, QPK, HD)
    context = attend(query_rows, kv_cache, fresh, row_lengths)
    layer_out = column_block.reshape(1, KVH, piece_cols, D)
    return (context, layer_out)


def flip(index, mask, size):
    result, bit = 0, 1
    while bit < size:
        value = (index // bit) % 2
        if mask & bit:
            value = 1 - value
        result = result + value * bit
        bit *= 2
    return result


def move_kernel(sections, shards, source_ref, train_ref, hidden_ref, query_ref, cache_ref, length_ref, out_ref, context_ref, *scratch):
    spread = scratch[:shards]
    (stage, picked, feat, part, part_send, part_recv,
     a_send, a_recv, b_send, b_recv, c_send, c_recv, h_send, h_recv, p_send, p_recv, local, w_ref, raw, raw_sem, held, held_max, held_sum) = scratch[shards:]
    me = lax.axis_index("section")
    pos = lax.axis_index("shard")
    heads, _, piece, width = w_ref.shape
    rows_in = hidden_ref.shape[0]
    per_head = shards // heads
    row_block = ROWS // per_head

    lanes = raw.shape[-1]
    together = lanes // piece
    groups = shards // together

    def group_of(i):
        return flip(pos // together, groups - 1 - i, groups)

    def load_copy(i, h):
        start = pl.multiple_of((h * groups + group_of(i)) * lanes, lanes)
        return pltpu.make_async_copy(train_ref.at[:, pl.ds(start, lanes)], raw.at[i, h], raw_sem.at[i, h])

    def turn(i, h):
        load_copy(i, h).wait()
        block = raw[i, h].astype(jnp.bfloat16).T
        w_ref[h, pl.ds(group_of(i) * together, together)] = block.reshape(together, piece, width)

    for i in range(groups):
        for h in range(heads):
            load_copy(i, h).start()

    barrier = pltpu.get_barrier_semaphore()
    for j in range(1, sections):
        pl.semaphore_signal(barrier, inc=1, device_id={"section": flip(me, j, sections)}, device_id_type=pl.DeviceIdType.MESH)
    for j in range(1, shards):
        pl.semaphore_signal(barrier, inc=1, device_id={"shard": flip(pos, j, shards)}, device_id_type=pl.DeviceIdType.MESH)
    pl.semaphore_wait(barrier, sections + shards - 2)

    def remote(src, dst, send, recv, **target):
        return pltpu.make_async_remote_copy(
            src_ref=src, dst_ref=dst, send_sem=send, recv_sem=recv,
            device_id=target, device_id_type=pl.DeviceIdType.MESH)

    masks = list(range(shards - 1, -1, -1))

    def spread_copies(k):
        p = flip(pos, masks[k], shards)
        copies = []
        for j in range(1, sections):
            t = flip(me, j, sections)
            copies.append(remote(w_ref.at[t, p], spread[k].at[me], a_send.at[k, j], a_recv.at[k, j], section=t))
        return copies

    def collect_copies(k):
        copies = []
        for j in range(1, sections):
            t = flip(me, j, sections)
            copies.append(remote(stage.at[k, t], picked.at[k, me], b_send.at[k, j], b_recv.at[k, j], section=t))
        return copies

    columns = pl.ds(pl.multiple_of(pos * width, width), width)

    def keep_copy(k):
        p = flip(pos, masks[k], shards)
        if masks[k] == 0:
            return pltpu.make_async_copy(picked.at[k], out_ref.at[:, :, columns], local)
        return remote(picked.at[k], out_ref.at[:, :, columns], c_send.at[k], c_recv.at[k], shard=p)

    def hidden_copy(j):
        p = flip(pos, j, shards)
        return remote(hidden_ref.at[:, pl.ds(pl.multiple_of(p * width, width), width)], feat.at[pos],
                      h_send.at[j], h_recv.at[j], shard=p)

    def start_spread(k):
        for copy in spread_copies(k):
            copy.start()
        spread[k][me] = w_ref[me, flip(pos, masks[k], shards)]

    ahead = AHEAD
    for j in range(shards - 1, 0, -1):
        hidden_copy(j).start()
    for h in range(heads):
        turn(0, h)
    for k in range(min(ahead, shards)):
        start_spread(k)
    feat[pos] = hidden_ref[:, columns]

    def collect(k):
        for copy in spread_copies(k):
            copy.wait()
        for g in range(sections):
            stage[k, g] = spread[k][source_ref[g]]
        picked[k, me] = stage[k, me]
        for copy in collect_copies(k):
            copy.start()

    def forward(k):
        for copy in collect_copies(k):
            copy.wait()
        keep_copy(k).start()

    def multiply(k):
        if k == 0:
            for j in range(1, shards):
                hidden_copy(j).wait()
        p = flip(pos, masks[k], shards)
        value = lax.dot_general(
            picked[k].reshape(heads * piece, width), feat[...].reshape(shards * rows_in, width),
            (((1,), (1,)), ((), ())), preferred_element_type=jnp.float32)
        for h in range(heads):
            part[h, pl.ds(pl.multiple_of(p * piece, piece), piece), :] = value[h * piece:(h + 1) * piece]

    scale = 1.0 / math.sqrt(HD)
    some = cache_ref.shape[0] // shards

    def attend_cached(k):
        rows = slice(k * some, (k + 1) * some)
        cache = cache_ref[rows]
        scores = lax.dot_general(query_ref[rows], cache[:, :, :HD], (((2,), (2,)), ((0,), (0,))),
                                 preferred_element_type=jnp.float32) * scale
        valid = lax.broadcasted_iota(jnp.int32, scores.shape, 2) < length_ref[rows]
        scores = jnp.where(valid, scores, -1e30)
        highest = jnp.max(scores, axis=-1, keepdims=True)
        weights = jnp.where(valid, jnp.exp(scores - highest), 0.0)
        held[rows] = lax.dot_general(weights.astype(jnp.bfloat16), cache[:, :, HD:], (((2,), (1,)), ((0,), (0,))),
                                     preferred_element_type=jnp.float32)
        held_max[rows] = jnp.broadcast_to(highest, scores.shape)
        held_sum[rows] = jnp.broadcast_to(jnp.sum(weights, axis=-1, keepdims=True), scores.shape)

    def attend_fresh(k, fresh):
        rows = slice(k * some, (k + 1) * some)
        key, value = fresh[rows, :HD][:, None, :], fresh[rows, HD:][:, None, :]
        score = jnp.sum(query_ref[rows].astype(jnp.float32) * key, axis=-1, keepdims=True) * scale
        highest = jnp.maximum(held_max[rows], score)
        old = jnp.exp(held_max[rows] - highest)
        new = jnp.exp(score - highest)
        total = held_sum[rows] * old + new
        prob = (new / total).astype(jnp.bfloat16).astype(jnp.float32)
        context_ref[rows] = (held[rows] * (old / total) + prob * value).astype(context_ref.dtype)

    for k in range(shards):
        if k >= 1:
            forward(k - 1)
        collect(k)
        if k + ahead < shards:
            start_spread(k + ahead)
        if k < groups - 1:
            for h in range(heads):
                turn(k + 1, h)
        if k >= 1:
            multiply(k - 1)
        attend_cached(k)
    forward(shards - 1)
    multiply(shards - 1)

    for h in range(heads):
        turned = part[h].T
        for b in range(per_head):
            part_send[h * per_head + b] = turned[b * row_block:(b + 1) * row_block]

    def part_copy(j):
        p = flip(pos, j, shards)
        return remote(part_send.at[p], part_recv.at[j], p_send.at[j], p_recv.at[j], shard=p)

    for j in range(shards - 1, 0, -1):
        part_copy(j).start()
    total = part_send[pos]
    for j in range(1, shards):
        part_copy(j).wait()
        total = total + part_recv[j]
    fresh = total.astype(jnp.bfloat16).astype(jnp.float32)
    for k in range(shards):
        attend_fresh(k, fresh)
    for k in range(shards):
        keep_copy(k).wait()


AHEAD = 1
LANES = 128


def move(weights, hidden, source, queries, cache, row_lengths):
    sections, shards = lax.axis_size("section"), lax.axis_size("shard")
    heads, piece, width = KVH, 2 * HD // shards, weights.shape[0]
    rows_in = hidden.shape[0]
    row_block = ROWS * heads // shards
    entries = cache.shape[0]
    lengths = jnp.broadcast_to(row_lengths[:, None, None], (entries, 1, LEN))
    vmem = pl.BlockSpec(memory_space=pltpu.VMEM)
    dma = pltpu.SemaphoreType.DMA
    return pl.pallas_call(
        functools.partial(move_kernel, sections, shards),
        out_shape=(
            jax.ShapeDtypeStruct((heads, piece, shards * width), jnp.bfloat16),
            jax.ShapeDtypeStruct((entries, QPK, HD), jnp.bfloat16),
        ),
        in_specs=[pl.BlockSpec(memory_space=pltpu.SMEM), pl.BlockSpec(memory_space=pl.ANY), vmem, vmem, vmem, vmem],
        out_specs=(pl.BlockSpec(memory_space=pl.ANY), vmem),
        scratch_shapes=[pltpu.VMEM((sections, piece, width), jnp.bfloat16)] * shards + [
            pltpu.VMEM((shards, sections, piece, width), jnp.bfloat16),
            pltpu.VMEM((shards, heads, piece, width), jnp.bfloat16),
            pltpu.VMEM((shards, rows_in, width), jnp.bfloat16),
            pltpu.VMEM((heads, 2 * HD, ROWS), jnp.float32),
            pltpu.VMEM((shards, row_block, 2 * HD), jnp.float32),
            pltpu.VMEM((shards, row_block, 2 * HD), jnp.float32),
            dma((shards, sections)), dma((shards, sections)),
            dma((shards, sections)), dma((shards, sections)),
            dma((shards,)), dma((shards,)), dma((shards,)), dma((shards,)), dma((shards,)), dma((shards,)),
            dma(()),
            pltpu.VMEM((heads, shards, piece, width), jnp.bfloat16),
            pltpu.VMEM((shards * piece // LANES, heads, width, LANES), jnp.float32),
            dma((shards * piece // LANES, heads)),
        ] + [pltpu.VMEM((entries, QPK, HD), jnp.float32)] * 3,
        compiler_params=pltpu.CompilerParams(
            collective_id=0, has_side_effects=True, vmem_limit_bytes=50 * 2**20),
        cost_estimate=pl.CostEstimate(flops=2 * ROWS * width * heads * piece * shards, bytes_accessed=4 * weights.size, transcendentals=0),
    )(source, weights, hidden, queries.reshape(entries, QPK, HD), cache, lengths)


def chunk_body(train_weights, section_to_group, hidden, queries, kv_cache, lengths):
    shards = lax.axis_size("shard")
    per_head = shards // KVH
    row_block = ROWS // per_head
    source = jnp.argsort(section_to_group).astype(jnp.int32)
    block = lax.axis_index("shard") % per_head
    row_lengths = lax.dynamic_slice_in_dim(lengths, block * row_block, row_block, 0)
    kept, context = move(train_weights[0], hidden, source, queries, kv_cache, row_lengths)
    context = context.reshape(queries.shape)
    return (context, kept[None])


def solution(mesh):
    sections, shards = mesh.shape["section"], mesh.shape["shard"]
    chunked = (
        sections == KVH and shards % KVH == 0 and shards & (shards - 1) == 0
        and (2 * HD // shards) % 16 == 0 and LANES % (2 * HD // shards) == 0 and (ROWS // shards) % 16 == 0
    )
    body = chunk_body if chunked else plain_body
    return jax.shard_map(
        body,
        mesh=mesh,
        in_specs=(
            P("section", "shard", None),
            P(),
            P(("section", "shard"), None),
            P(("section", "shard"), None),
            P(("section", "shard"), None, None),
            P("section"),
        ),
        out_specs=(P(("section", "shard"), None), P("section", None, "shard", None)),
        check_vma=False,
    )
```
